512 devices in a mesh: dp: 16 (over y, core), seq: 32 (over x, z).
Axes of the slice: x: 4, y: 8, z: 8, core: 2. Of those that a mesh axis runs over, the one named last changes fastest.
Arguments:
- queries: bfloat16 [65536, 8192], P(('dp', 'seq')), may hold values from -8 to 8
- keys: bfloat16 [65536, 1024], P(('dp', 'seq')), may hold values from -8 to 8
- values: bfloat16 [65536, 1024], P(('dp', 'seq')), may hold values from -6 to 6
- doc_ids: int32 [65536], P(('dp', 'seq')), may hold values from 0 to 511, never falling along the last dimension, each value on 1 to 512 neighbouring positions
Outputs:
- attended: bfloat16 [65536, 8192], P(('dp', 'seq'))
The draws below stay inside these ranges and needn't reach their ends.
Inputs may be any that keep to these rules, and one draw needn't show every extreme that they name: `doc_ids`: document ids never fall along the tokens; each document is 1 to 512 consecutive tokens, and some document has exactly 512.
All inputs are finite; a program needn't handle non-finite values.
Results may differ from the reference program's by a relative error of at most 0.0031.
Values may be sent and summed in bfloat16 or wider, within the bound.
A program may use at most 64 MiB of HBM per device.

```python
import math
import jax
import jax.numpy as jnp
import numpy as np
from jax import lax

QUERY_HEADS = 64
KEY_VALUE_HEADS = 8
HEAD_SIZE = 128
LONGEST_DOCUMENT = 512
QBLOCK = 512
WINDOW_TOKENS = 65536


def draw_queries(key, part):
    key = jax.random.fold_in(key, 11)
    return jax.random.truncated_normal(key, -6.0, 6.0, (WINDOW_TOKENS, QUERY_HEADS * HEAD_SIZE), jnp.float32).astype(jnp.bfloat16)


def draw_keys(key, part):
    key = jax.random.fold_in(key, 23)
    return jax.random.truncated_normal(key, -6.0, 6.0, (WINDOW_TOKENS, KEY_VALUE_HEADS * HEAD_SIZE), jnp.float32).astype(jnp.bfloat16)


def shard_levels(key, extent, cuts, least, largest):
    gain = 1.0
    for position, parts in cuts:
        heights = jax.random.uniform(jax.random.fold_in(jax.random.fold_in(key, 6), position), (parts,), jnp.float32, least / len(cuts), largest / len(cuts))
        gain = gain * jnp.repeat(jnp.exp(heights), extent[position] // parts).reshape((-1,) + (1,) * (len(extent) - 1 - position))
    return gain


def split_up(amount, total, most, skew):
    portions = [(1 << 20) // math.isqrt(rank ** skew) + 1 for rank in range(2, amount + 1)]
    surplus, holding = total - most - (amount - 1), [1] * (amount - 1)
    while surplus > 0:
        candidates = [i for i in range(amount - 1) if holding[i] < most]
        pool, budget = sum([portions[i] for i in candidates]), surplus
        for i in candidates:
            addition = min(most - holding[i], max(1, budget * portions[i] // pool), surplus)
            holding[i] = holding[i] + addition
            surplus = surplus - addition
    return np.array([most] + holding)


def ragged_sizes(own_key, count, total, bound, slope):
    if count == 2:
        one = jax.random.randint(own_key, (), max(1, total - bound), min(bound, total - 1) + 1)
        return jnp.stack([one, total - one])
    sizes = jnp.asarray(split_up(count, total, bound, slope), jnp.int32)
    pairs = (count - 1) // 2
    donor, sink = sizes[1:1 + 2 * pairs:2], sizes[2:2 + 2 * pairs:2]
    margin = jnp.minimum(donor - 1, bound - sink)
    moved = jax.random.randint(jax.random.fold_in(own_key, 1), (pairs,), 0, 1 << 20) % (margin + 1)
    sizes = sizes.at[1:1 + 2 * pairs:2].set(donor - moved).at[2:2 + 2 * pairs:2].set(sink + moved)
    return sizes[jax.random.permutation(jax.random.fold_in(own_key, 2), count)]


def normal_values(stream_key, shape, deviation, limit, cuts=(), kind=jnp.bfloat16):
    values = jax.random.normal(stream_key, shape, jnp.float32) * deviation
    if len(cuts) > 0:
        values = shard_levels(stream_key, shape, cuts, -0.22, 0.18) * values
    return jnp.clip(values, min=-limit, max=limit).astype(kind)


def setup_inputs(seed: int = 0) -> dict:
    key_list = jax.random.split(jax.random.key(seed), 5)
    queries = draw_queries(jax.random.fold_in(key_list[4], 71), 0)
    keys = draw_keys(jax.random.fold_in(key_list[4], 71), 0)
    values = normal_values(key_list[2], (WINDOW_TOKENS, KEY_VALUE_HEADS * HEAD_SIZE), 1.0, 6.0, ((0, 512),))
    doc_ids = jnp.searchsorted(jnp.cumsum(ragged_sizes(key_list[3], 4 * WINDOW_TOKENS // LONGEST_DOCUMENT, WINDOW_TOKENS, LONGEST_DOCUMENT, 2)), jnp.arange(WINDOW_TOKENS), side="right").astype(jnp.int32)
    return {"queries": queries, "keys": keys, "values": values, "doc_ids": doc_ids}


def reference(queries, keys, values, doc_ids):
    group_width = QUERY_HEADS // KEY_VALUE_HEADS
    score_scale = HEAD_SIZE ** -0.5
    query_heads = queries.reshape(WINDOW_TOKENS, QUERY_HEADS, HEAD_SIZE)
    key_head_rows = jnp.concatenate([jnp.zeros((LONGEST_DOCUMENT, KEY_VALUE_HEADS * HEAD_SIZE), jnp.bfloat16), keys], axis=0).reshape(LONGEST_DOCUMENT + WINDOW_TOKENS, KEY_VALUE_HEADS, HEAD_SIZE)
    value_head_rows = jnp.concatenate([jnp.zeros((LONGEST_DOCUMENT, KEY_VALUE_HEADS * HEAD_SIZE), jnp.bfloat16), values], axis=0).reshape(LONGEST_DOCUMENT + WINDOW_TOKENS, KEY_VALUE_HEADS, HEAD_SIZE)
    doc_padded = jnp.concatenate([jnp.full((LONGEST_DOCUMENT,), -1, jnp.int32), doc_ids.astype(jnp.int32)], axis=0)
    block_count = WINDOW_TOKENS // QBLOCK

    def per_head(head_index):
        pair_index = (head_index // group_width).astype(jnp.int32)
        query_all = lax.dynamic_index_in_dim(query_heads, head_index, 1, keepdims=False)
        key_all = lax.dynamic_index_in_dim(key_head_rows, pair_index, 1, keepdims=False)
        value_all = lax.dynamic_index_in_dim(value_head_rows, pair_index, 1, keepdims=False)

        def per_block(block_index):
            offset = (block_index * QBLOCK).astype(jnp.int32)
            query_block = lax.dynamic_slice_in_dim(query_all, offset, QBLOCK, 0)
            key_window = lax.dynamic_slice_in_dim(key_all, offset, LONGEST_DOCUMENT + QBLOCK, 0)
            value_window = lax.dynamic_slice_in_dim(value_all, offset, LONGEST_DOCUMENT + QBLOCK, 0)
            key_docs = lax.dynamic_slice_in_dim(doc_padded, offset, LONGEST_DOCUMENT + QBLOCK, 0)
            query_docs = lax.dynamic_slice_in_dim(doc_padded, offset + LONGEST_DOCUMENT, QBLOCK, 0)
            scores = jnp.dot(query_block, key_window.T, preferred_element_type=jnp.float32) * score_scale
            query_pos = offset + LONGEST_DOCUMENT + jnp.arange(QBLOCK, dtype=jnp.int32)
            key_pos = offset + jnp.arange(LONGEST_DOCUMENT + QBLOCK, dtype=jnp.int32)
            allowed = (query_docs[:, None] == key_docs[None, :]) & (key_pos[None, :] <= query_pos[:, None])
            scores = jnp.where(allowed, scores, -jnp.inf)
            row_max = jnp.max(scores, axis=1, keepdims=True)
            weight = jnp.exp(scores - row_max)
            totals = jnp.sum(weight, axis=1, keepdims=True)
            mixed_out = jnp.dot(weight.astype(jnp.bfloat16), value_window, preferred_element_type=jnp.float32) / totals
            return mixed_out.astype(jnp.bfloat16)

        return lax.map(per_block, jnp.arange(block_count, dtype=jnp.int32)).reshape(WINDOW_TOKENS, HEAD_SIZE)

    per_heads = lax.map(per_head, jnp.arange(QUERY_HEADS, dtype=jnp.int32))
    return jnp.transpose(per_heads, (1, 0, 2)).reshape(WINDOW_TOKENS, QUERY_HEADS * HEAD_SIZE)
```

```python
import functools

import jax
import jax.numpy as jnp
from jax import lax
from jax.experimental import pallas as pl
from jax.experimental.pallas import tpu as pltpu
from jax.sharding import PartitionSpec as P

QUERY_HEADS = 64
KEY_VALUE_HEADS = 8
GROUP = QUERY_HEADS // KEY_VALUE_HEADS
HEAD_SIZE = 128
LONGEST_DOCUMENT = 512
MESH = pl.DeviceIdType.MESH
SCORE_SCALE = HEAD_SIZE**-0.5 * 1.4426950408889634

PLUS_HEADS = 5
REACH = 4
PLUS, MINUS = 0, 1


def arrivals(hop_us, latency_us, jump_hops):
    order = []
    for way, heads in ((PLUS, range(PLUS_HEADS)), (MINUS, range(PLUS_HEADS, KEY_VALUE_HEADS))):
        stages = range(1, REACH + 1) if way == PLUS else range(REACH + 1, 0, -1)
        clock, ready = 0.0, {head: 0.0 for head in heads}
        for distance in stages:
            for head in heads:
                clock = max(clock, ready[head]) + hop_us * (jump_hops if distance > REACH else 1)
                ready[head] = clock + latency_us
                order.append((ready[head], way, distance, head))
    return sorted(order)


def kernel(
    seq_size, device_count, order, queries, keys, values, docs, out,
    pairs, transit, query_rows, doc_rows, bias,
    local_sem, query_sem, send_sem, recv_sem, doc_send, doc_recv,
):
    me = lax.axis_index("dp") * seq_size + lax.axis_index("seq")

    def block_device(step):
        block = lax.rem(me + (step + device_count), device_count)
        return (block // seq_size, lax.rem(block, seq_size))

    right, left, ahead, behind = (block_device(s) for s in (1, -1, REACH + 1, -REACH - 1))
    barrier = pltpu.get_barrier_semaphore()
    for device in (right, left, behind):
        pl.semaphore_signal(barrier, inc=1, device_id=device, device_id_type=MESH)
    own = []
    for head in [*range(PLUS_HEADS, KEY_VALUE_HEADS), *range(PLUS_HEADS)]:
        for part, ref in enumerate((keys, values)):
            columns = ref.at[:, pl.ds(head * HEAD_SIZE, HEAD_SIZE)]
            own.append(pltpu.make_async_copy(columns, pairs.at[0, head, part], local_sem.at[head, part]))
            own[-1].start()
    query_copy = pltpu.make_async_copy(queries, query_rows, query_sem)
    query_copy.start()
    doc_rows[0] = jnp.broadcast_to(docs[...], doc_rows.shape[1:])
    for copy in own:
        copy.wait()
    pl.semaphore_wait(barrier, 3)

    def remote(source, target, sent, received, device):
        return pltpu.make_async_remote_copy(
            src_ref=source, dst_ref=target, send_sem=sent, recv_sem=received, device_id=device, device_id_type=MESH
        )

    copies = {}

    def send(way, distance, head):
        sems = (send_sem.at[distance - 1, head], recv_sem.at[distance - 1, head])
        if way == PLUS:
            copy = remote(pairs.at[distance - 1, head], pairs.at[distance, head], *sems, right)
        elif distance > REACH:
            copy = remote(pairs.at[0, head], transit.at[head - PLUS_HEADS], *sems, ahead)
        else:
            source = transit.at[head - PLUS_HEADS] if distance == REACH else pairs.at[distance + 1, head]
            copy = remote(source, pairs.at[distance, head], *sems, left)
        copy.start()
        copies[way, distance, head] = copy

    def doc_copy(distance):
        return remote(
            doc_rows.at[distance - 1], doc_rows.at[distance], doc_send.at[distance - 1], doc_recv.at[distance - 1], right
        )

    def attend(head):
        key_rows = jnp.concatenate([pairs[d, head, 0] for d in range(REACH + 1)], axis=0)
        value_rows = jnp.concatenate([pairs[d, head, 1] for d in range(REACH + 1)], axis=0)
        first = head * GROUP * HEAD_SIZE
        tokens = query_rows.shape[0]
        rows = jnp.concatenate(
            [query_rows[:, first + g * HEAD_SIZE : first + (g + 1) * HEAD_SIZE] for g in range(GROUP)], axis=0
        )
        scores = lax.dot_general(rows, key_rows, (((1,), (1,)), ((), ())), preferred_element_type=jnp.float32)
        scores = (scores * SCORE_SCALE).reshape(GROUP, tokens, -1) + bias[...][None]
        scores = scores.reshape(GROUP * tokens, -1)
        row_max = jnp.max(scores, axis=1, keepdims=True)
        weight = jnp.exp2(scores - row_max)
        totals = jnp.sum(weight, axis=1, keepdims=True)
        mixed = lax.dot_general(
            weight.astype(jnp.bfloat16), value_rows, (((1,), (0,)), ((), ())), preferred_element_type=jnp.float32
        )
        mixed = (mixed / totals).astype(jnp.bfloat16)
        for g in range(GROUP):
            out[:, first + g * HEAD_SIZE : first + (g + 1) * HEAD_SIZE] = mixed[g * tokens : (g + 1) * tokens]

    def fill_bias():
        tokens = query_rows.shape[0]
        query_docs = jnp.broadcast_to(docs[...], (tokens, tokens)).T
        for distance in range(REACH + 1):
            same = jnp.broadcast_to(doc_rows[distance, 0:1], (tokens, tokens)) == query_docs
            if distance == 0:
                row = lax.broadcasted_iota(jnp.int32, (tokens, tokens), 0)
                column = lax.broadcasted_iota(jnp.int32, (tokens, tokens), 1)
                same = same & (column <= row)
            else:
                same = same & (jnp.full((tokens, tokens), me, jnp.int32) >= distance)
            bias[:, distance * tokens : (distance + 1) * tokens] = jnp.where(same, 0.0, -jnp.inf)

    doc_copy(1).start()
    for head in range(PLUS_HEADS, KEY_VALUE_HEADS):
        send(MINUS, REACH + 1, head)
    for head in range(PLUS_HEADS):
        send(PLUS, 1, head)
    ready = []
    for position, (_, way, distance, head) in enumerate(order):
        if position % 3 == 2 and position // 3 < REACH:
            doc_distance = position // 3 + 1
            doc_copy(doc_distance).wait_recv()
            if doc_distance < REACH:
                doc_copy(doc_distance + 1).start()
            else:
                fill_bias()
                query_copy.wait()
        copies[way, distance, head].wait_recv()
        if way == PLUS and distance < REACH:
            send(PLUS, distance + 1, head)
        elif way == MINUS and distance > 1:
            send(MINUS, distance - 1, head)
        else:
            ready.append(head)
        if not any((w == PLUS and d < REACH) or (w == MINUS and d > 1) for _, w, d, _ in order[position + 1 :]):
            for done in ready:
                attend(done)
            ready = []
    for copy in copies.values():
        copy.wait_send()
    for distance in range(1, REACH + 1):
        doc_copy(distance).wait_send()


def on_device(seq_size, device_count, queries, keys, values, doc_ids):
    tokens = queries.shape[0]
    order = arrivals(1.38, 2.5, 1.5)
    pair = (tokens, HEAD_SIZE)
    links = (REACH + 1, KEY_VALUE_HEADS)
    return pl.pallas_call(
        functools.partial(kernel, seq_size, device_count, order),
        out_shape=jax.ShapeDtypeStruct(queries.shape, jnp.bfloat16),
        in_specs=[
            pl.BlockSpec(memory_space=pl.ANY),
            pl.BlockSpec(memory_space=pl.ANY),
            pl.BlockSpec(memory_space=pl.ANY),
            pl.BlockSpec(memory_space=pltpu.VMEM),
        ],
        out_specs=pl.BlockSpec(memory_space=pltpu.VMEM),
        scratch_shapes=[
            pltpu.VMEM((REACH + 1, KEY_VALUE_HEADS, 2, *pair), jnp.bfloat16),
            pltpu.VMEM((KEY_VALUE_HEADS - PLUS_HEADS, 2, *pair), jnp.bfloat16),
            pltpu.VMEM(queries.shape, jnp.bfloat16),
            pltpu.VMEM((REACH + 1, 8, tokens), jnp.int32),
            pltpu.VMEM((tokens, (REACH + 1) * tokens), jnp.float32),
            pltpu.SemaphoreType.DMA((KEY_VALUE_HEADS, 2)),
            pltpu.SemaphoreType.DMA,
            pltpu.SemaphoreType.DMA(links),
            pltpu.SemaphoreType.DMA(links),
            pltpu.SemaphoreType.DMA((REACH,)),
            pltpu.SemaphoreType.DMA((REACH,)),
        ],
        compiler_params=pltpu.CompilerParams(
            collective_id=0, has_side_effects=True, vmem_limit_bytes=60 * 1024 * 1024
        ),
    )(queries, keys, values, doc_ids.reshape(1, tokens))


def solution(mesh):
    seq_size = mesh.shape["seq"]
    spec = P(("dp", "seq"), None)
    return jax.shard_map(
        functools.partial(on_device, seq_size, mesh.shape["dp"] * seq_size),
        mesh=mesh,
        in_specs=(spec, spec, spec, P(("dp", "seq"))),
        out_specs=spec,
        check_vma=False,
    )
```

```python
import functools

import jax
import jax.numpy as jnp
from jax import lax
from jax.experimental import pallas as pl
from jax.experimental.pallas import tpu as pltpu
from jax.sharding import PartitionSpec as P

QUERY_HEADS = 64
KEY_VALUE_HEADS = 8
GROUP = QUERY_HEADS // KEY_VALUE_HEADS
HEAD_SIZE = 128
LONGEST_DOCUMENT = 512
VMEM_BYTES = 40 << 20
HOLD = 1
LINE = 8
TIMES = (((3.9, 1.4), (7.0, 1.4, 4.2, 0.0), 3.0), ((3.9, 1.4), (7.0, 1.4, 4.2, 6.0), 3.0))


def own_first(dp, seq):
    return lax.rem(seq, LINE) < 3


MESH = pl.DeviceIdType.MESH
SCORE_SCALE = HEAD_SIZE**-0.5 * 1.4426950408889634

PLUS_HEADS = 5
REACH = 4
PLUS, MINUS = 0, 1
EARLY_BLOCKS = {PLUS: (1, 2), MINUS: (4, 3)}
LATE_BLOCKS = {PLUS: (3, 4), MINUS: (2, 1)}
EARLY_END = {(way, blocks[-1]) for way, blocks in EARLY_BLOCKS.items()}
LATE_END = {(way, blocks[-1]) for way, blocks in LATE_BLOCKS.items()}


def schedule(plus, minus, doc):
    steps = [(doc * distance, "doc", distance) for distance in range(1, REACH + 1)]
    for stage in range(REACH):
        for head in range(PLUS_HEADS):
            steps.append((plus[0] + plus[1] * (stage * PLUS_HEADS + head), "block", PLUS, stage + 1, head))
    for stage in range(REACH + 1):
        for index, head in enumerate(range(PLUS_HEADS, KEY_VALUE_HEADS)):
            steps.append((minus[0] + minus[1] * index + minus[2] * stage + (minus[3] if stage else 0.0), "block", MINUS, REACH + 1 - stage, head))
    return sorted(steps)


def kernel(
    seq_size, device_count, orders, queries, keys, values, docs, out,
    pairs, transit, query_rows, doc_rows, bias, top, total, partial,
    local_sem, query_sem, send_sem, recv_sem, doc_send, doc_recv,
):
    me = lax.axis_index("dp") * seq_size + lax.axis_index("seq")

    def block_device(step):
        block = lax.rem(me + (step + device_count), device_count)
        return (block // seq_size, lax.rem(block, seq_size))

    right, left, ahead, behind = (block_device(s) for s in (1, -1, REACH + 1, -REACH - 1))
    greet = (right, left, behind)
    barrier = pltpu.get_barrier_semaphore()
    for device in greet:
        pl.semaphore_signal(barrier, inc=1, device_id=device, device_id_type=MESH)
    own = []
    for head in [*range(PLUS_HEADS, KEY_VALUE_HEADS), *range(PLUS_HEADS)]:
        for part, ref in enumerate((keys, values)):
            columns = ref.at[:, pl.ds(head * HEAD_SIZE, HEAD_SIZE)]
            own.append(pltpu.make_async_copy(columns, pairs.at[0, head, part], local_sem.at[head, part]))
            own[-1].start()
    query_copy = pltpu.make_async_copy(queries, query_rows, query_sem)
    query_copy.start()
    doc_rows[0] = jnp.broadcast_to(docs[...], doc_rows.shape[1:])
    for copy in own:
        copy.wait()

    def remote(source, target, sent, received, device):
        return pltpu.make_async_remote_copy(
            src_ref=source, dst_ref=target, send_sem=sent, recv_sem=received, device_id=device, device_id_type=MESH
        )

    def block_copy(way, distance, head):
        sems = (send_sem.at[distance - 1, head], recv_sem.at[distance - 1, head])
        if way == PLUS:
            return remote(pairs.at[distance - 1, head], pairs.at[distance, head], *sems, right)
        if distance > REACH:
            return remote(pairs.at[0, head], transit.at[head - PLUS_HEADS], *sems, ahead)
        source = transit.at[head - PLUS_HEADS] if distance == REACH else pairs.at[distance + 1, head]
        return remote(source, pairs.at[distance, head], *sems, left)

    def doc_copy(distance):
        return remote(
            doc_rows.at[distance - 1], doc_rows.at[distance], doc_send.at[distance - 1], doc_recv.at[distance - 1], right
        )

    def attend(head, blocks, first, last):
        tokens = query_rows.shape[0]
        key_rows = jnp.concatenate([pairs[d, head, 0] for d in blocks], axis=0)
        value_rows = jnp.concatenate([pairs[d, head, 1] for d in blocks], axis=0)
        mask = jnp.concatenate([bias[d] for d in blocks], axis=0)
        columns = [pl.ds(pl.multiple_of((head * GROUP + g) * HEAD_SIZE, HEAD_SIZE), HEAD_SIZE) for g in range(GROUP)]
        rows = jnp.concatenate([query_rows[:, column] for column in columns], axis=0)
        scores = lax.dot_general(key_rows, rows, (((1,), (1,)), ((), ())), preferred_element_type=jnp.float32)
        scores = scores * SCORE_SCALE + jnp.concatenate([mask] * GROUP, axis=1)
        highest = jnp.max(scores, axis=0, keepdims=True)
        if not first:
            highest = jnp.maximum(highest, top[head])
        weight = jnp.exp2(scores - highest)
        sums = jnp.sum(weight, axis=0, keepdims=True)
        mixed = lax.dot_general(
            value_rows, weight.astype(jnp.bfloat16), (((0,), (0,)), ((), ())), preferred_element_type=jnp.float32
        )
        if not first:
            shrink = jnp.exp2(top[head] - highest)
            sums = sums + total[head] * shrink
            mixed = mixed + partial[head] * shrink
        if not last:
            top[head], total[head], partial[head] = highest, sums, mixed
            return
        mixed = mixed / sums
        for g, column in enumerate(columns):
            out[:, column] = mixed[:, g * tokens : (g + 1) * tokens].T.astype(jnp.bfloat16)

    def fill_bias(distance):
        tokens = query_rows.shape[0]
        square = (tokens, tokens)
        same = jnp.broadcast_to(doc_rows[distance, 0:1], square).T == jnp.broadcast_to(docs[...], square)
        if distance == 0:
            key, query = (lax.broadcasted_iota(jnp.int32, square, axis) for axis in (0, 1))
            same = same & (key <= query)
        else:
            same = same & (jnp.full(square, me, jnp.int32) >= distance)
        bias[distance] = jnp.where(same, 0.0, -jnp.inf)

    def attend_own():
        query_copy.wait()
        fill_bias(0)
        pl.loop(0, KEY_VALUE_HEADS)(lambda head: attend(head, (0,), True, False))

    early = own_first(lax.axis_index("dp"), lax.axis_index("seq"))
    pl.when(early)(attend_own)
    pl.semaphore_wait(barrier, len(greet))
    doc_copy(1).start()
    for head in range(PLUS_HEADS, KEY_VALUE_HEADS):
        block_copy(MINUS, REACH + 1, head).start()
    for head in range(PLUS_HEADS):
        block_copy(PLUS, 1, head).start()
    pl.when(jnp.logical_not(early))(attend_own)
    def follow(order):
        work, waiting = [], HOLD
        for step in order:
            if step[1] == "doc":
                doc_copy(step[2]).wait_recv()
                if step[2] < REACH:
                    doc_copy(step[2] + 1).start()
                fill_bias(step[2])
                waiting = 0 if step[2] == REACH else waiting
                continue
            way, distance, head = step[2:]
            block_copy(way, distance, head).wait_recv()
            if way == PLUS and distance < REACH:
                block_copy(PLUS, distance + 1, head).start()
            elif way == MINUS and distance > 1:
                block_copy(MINUS, distance - 1, head).start()
            if (way, distance) in EARLY_END:
                work.append((head, EARLY_BLOCKS[way], False, False))
            if (way, distance) in LATE_END:
                work.append((head, LATE_BLOCKS[way], False, True))
            if work and not waiting:
                attend(*work.pop(0))
        for item in work:
            attend(*item)

    first_half = lax.rem(lax.axis_index("seq"), LINE) < LINE // 2
    pl.when(first_half)(lambda: follow(orders[0]))
    pl.when(jnp.logical_not(first_half))(lambda: follow(orders[1]))
    for way, distance, head in (step[2:] for step in orders[0] if step[1] == "block"):
        block_copy(way, distance, head).wait_send()
    for distance in range(1, REACH + 1):
        doc_copy(distance).wait_send()


def on_device(seq_size, device_count, queries, keys, values, doc_ids):
    tokens = queries.shape[0]
    orders = [schedule(*times) for times in TIMES]
    pair = (tokens, HEAD_SIZE)
    links = (REACH + 1, KEY_VALUE_HEADS)
    return pl.pallas_call(
        functools.partial(kernel, seq_size, device_count, orders),
        out_shape=jax.ShapeDtypeStruct(queries.shape, jnp.bfloat16),
        in_specs=[
            pl.BlockSpec(memory_space=pltpu.HBM),
            pl.BlockSpec(memory_space=pltpu.HBM),
            pl.BlockSpec(memory_space=pltpu.HBM),
            pl.BlockSpec(memory_space=pltpu.VMEM),
        ],
        out_specs=pl.BlockSpec(memory_space=pltpu.VMEM),
        scratch_shapes=[
            pltpu.VMEM((REACH + 1, KEY_VALUE_HEADS, 2, *pair), jnp.bfloat16),
            pltpu.VMEM((KEY_VALUE_HEADS - PLUS_HEADS, 2, *pair), jnp.bfloat16),
            pltpu.VMEM(queries.shape, jnp.bfloat16),
            pltpu.VMEM((REACH + 1, 8, tokens), jnp.int32),
            pltpu.VMEM((REACH + 1, tokens, tokens), jnp.float32),
            pltpu.VMEM((KEY_VALUE_HEADS, 1, GROUP * tokens), jnp.float32),
            pltpu.VMEM((KEY_VALUE_HEADS, 1, GROUP * tokens), jnp.float32),
            pltpu.VMEM((KEY_VALUE_HEADS, HEAD_SIZE, GROUP * tokens), jnp.float32),
            pltpu.SemaphoreType.DMA((KEY_VALUE_HEADS, 2)),
            pltpu.SemaphoreType.DMA,
            pltpu.SemaphoreType.DMA(links),
            pltpu.SemaphoreType.DMA(links),
            pltpu.SemaphoreType.DMA((REACH,)),
            pltpu.SemaphoreType.DMA((REACH,)),
        ],
        compiler_params=pltpu.CompilerParams(
            collective_id=0, has_side_effects=True, vmem_limit_bytes=VMEM_BYTES
        ),
    )(*(pltpu.with_memory_space_constraint(x, pltpu.HBM) for x in (queries, keys, values)), doc_ids.reshape(1, tokens))


def solution(mesh):
    seq_size = mesh.shape["seq"]
    spec = P(("dp", "seq"), None)
    return jax.shard_map(
        functools.partial(on_device, seq_size, mesh.shape["dp"] * seq_size),
        mesh=mesh,
        in_specs=(spec, spec, spec, P(("dp", "seq"))),
        out_specs=spec,
        check_vma=False,
    )
```

```python
import functools

import jax
import jax.numpy as jnp
from jax import lax
from jax.experimental import pallas as pl
from jax.experimental.pallas import tpu as pltpu
from jax.sharding import PartitionSpec as P

QUERY_HEADS = 64
KEY_VALUE_HEADS = 8
GROUP = QUERY_HEADS // KEY_VALUE_HEADS
HEAD_SIZE = 128
LONGEST_DOCUMENT = 512
VMEM_BYTES = 40 << 20
HOLD = 1
LINE = 8
TIMES = (((3.9, 1.4, 5.3), (7.0, 1.4, 4.2, 0.0), 8.0), ((3.9, 1.4, 6), (7.0, 1.4, 4.2, 3.0), 8.0))


def own_first(dp, seq):
    return lax.rem(seq, LINE) < 3


MESH = pl.DeviceIdType.MESH
SCORE_SCALE = HEAD_SIZE**-0.5 * 1.4426950408889634

ONWARD = (6, 5)
REACH = 4
PLUS, MINUS = 0, 1
STEPS = {PLUS: ((1, 2), (3, 4)), MINUS: ((4, 3), (2, 1))}
EITHER = (((4, 3), (2, 1)), ((2, 3), (1, 4)))


def sender_halves(half, distance):
    places = range(half * LINE // 2, (half + 1) * LINE // 2)
    return {(place - distance) % LINE * 2 // LINE for place in places}


def schedule(half, plus, minus, doc):
    steps = [(doc + 0.1 * distance, "doc", distance) for distance in range(1, REACH + 1)]
    for distance in range(1, REACH + 1):
        for head in range(max(ONWARD[sender] for sender in sender_halves(half, distance))):
            steps.append((plus[0] + plus[1] * ((distance - 1) * plus[2] + head), "block", PLUS, distance, head))
    for distance in range(1, REACH + 2):
        for head in range(min(ONWARD[sender] for sender in sender_halves(half, distance)), KEY_VALUE_HEADS):
            index, stage = KEY_VALUE_HEADS - 1 - head, REACH + 1 - distance
            time = minus[0] + minus[1] * index + minus[2] * stage + (minus[3] if stage else 0.0)
            steps.append((time, "block", MINUS, distance, head))
    return sorted(steps)


def kernel(
    seq_size, device_count, orders, queries, keys, values, docs, out,
    pairs, transit, query_rows, own_docs, doc_rows, bias, top, total, partial,
    local_sem, query_sem, doc_sem, send_sem, recv_sem, doc_send, doc_recv,
):
    me = lax.axis_index("dp") * seq_size + lax.axis_index("seq")

    def block_device(step):
        block = lax.rem(me + (step + device_count), device_count)
        return (block // seq_size, lax.rem(block, seq_size))

    right, left, ahead, behind = (block_device(s) for s in (1, -1, REACH + 1, -REACH - 1))
    greet = (right, left, behind, *(block_device(-distance) for distance in range(2, REACH + 1)))
    barrier = pltpu.get_barrier_semaphore()
    for device in greet:
        pl.semaphore_signal(barrier, inc=1, device_id=device, device_id_type=MESH)
    own = [pltpu.make_async_copy(docs, own_docs, doc_sem)]
    own[0].start()
    for head in reversed(range(KEY_VALUE_HEADS)):
        for part, ref in enumerate((keys, values)):
            columns = ref.at[:, pl.ds(head * HEAD_SIZE, HEAD_SIZE)]
            own.append(pltpu.make_async_copy(columns, pairs.at[0, head, part], local_sem.at[head, part]))
            own[-1].start()
    query_copy = pltpu.make_async_copy(queries, query_rows, query_sem)
    query_copy.start()
    for copy in own:
        copy.wait()
    doc_rows[0] = jnp.broadcast_to(own_docs[...], doc_rows.shape[1:])

    def remote(source, target, sent, received, device):
        return pltpu.make_async_remote_copy(
            src_ref=source, dst_ref=target, send_sem=sent, recv_sem=received, device_id=device, device_id_type=MESH
        )

    place = lax.rem(lax.axis_index("seq"), LINE)
    in_first_half = place < LINE // 2

    def by_way(half, way, distance, head, action):
        ways = {sender: PLUS if head < ONWARD[sender] else MINUS for sender in sender_halves(half, distance)}
        if set(ways.values()) == {way}:
            action()
        elif way in ways.values():
            first = lax.rem(place - distance + LINE, LINE) < LINE // 2
            pl.when(first if ways[0] == way else jnp.logical_not(first))(action)

    def block_copy(way, distance, head):
        sems = (send_sem.at[way, distance - 1, head], recv_sem.at[distance - 1, head])
        if way == PLUS:
            return remote(pairs.at[distance - 1, head], pairs.at[distance, head], *sems, right)
        if distance > REACH:
            return remote(pairs.at[0, head], transit.at[head - min(ONWARD)], *sems, ahead)
        source = transit.at[head - min(ONWARD)] if distance == REACH else pairs.at[distance + 1, head]
        return remote(source, pairs.at[distance, head], *sems, left)

    def doc_copy(distance):
        return remote(
            doc_rows.at[0], doc_rows.at[distance], doc_send.at[distance - 1], doc_recv.at[distance - 1], block_device(distance)
        )

    def attend(head, blocks, first, last):
        tokens = query_rows.shape[0]
        key_rows = jnp.concatenate([pairs[d, head, 0] for d in blocks], axis=0)
        value_rows = jnp.concatenate([pairs[d, head, 1] for d in blocks], axis=0)
        mask = jnp.concatenate([bias[d] for d in blocks], axis=0)
        columns = [pl.ds(pl.multiple_of((head * GROUP + g) * HEAD_SIZE, HEAD_SIZE), HEAD_SIZE) for g in range(GROUP)]
        rows = jnp.concatenate([query_rows[:, column] for column in columns], axis=0)
        scores = lax.dot_general(key_rows, rows, (((1,), (1,)), ((), ())), preferred_element_type=jnp.float32)
        scores = scores * SCORE_SCALE + jnp.concatenate([mask] * GROUP, axis=1)
        highest = jnp.max(scores, axis=0, keepdims=True)
        if not first:
            highest = jnp.maximum(highest, top[head])
        weight = jnp.exp2(scores - highest)
        sums = jnp.sum(weight, axis=0, keepdims=True)
        mixed = lax.dot_general(
            value_rows, weight.astype(jnp.bfloat16), (((0,), (0,)), ((), ())), preferred_element_type=jnp.float32
        )
        if not first:
            shrink = jnp.exp2(top[head] - highest)
            sums = sums + total[head] * shrink
            mixed = mixed + partial[head] * shrink
        if not last:
            top[head], total[head], partial[head] = highest, sums, mixed
            return
        mixed = mixed / sums
        for g, column in enumerate(columns):
            out[:, column] = mixed[:, g * tokens : (g + 1) * tokens].T.astype(jnp.bfloat16)

    def fill_bias(distance):
        tokens = query_rows.shape[0]
        square = (tokens, tokens)
        same = jnp.broadcast_to(doc_rows[distance, 0:1], square).T == jnp.broadcast_to(own_docs[...], square)
        if distance == 0:
            key, query = (lax.broadcasted_iota(jnp.int32, square, axis) for axis in (0, 1))
            same = same & (key <= query)
        else:
            same = same & (jnp.full(square, me, jnp.int32) >= distance)
        bias[distance] = jnp.where(same, 0.0, -jnp.inf)

    def attend_own():
        query_copy.wait()
        fill_bias(0)
        pl.loop(0, KEY_VALUE_HEADS)(lambda head: attend(head, (0,), True, False))

    early = own_first(lax.axis_index("dp"), lax.axis_index("seq"))
    pl.when(early)(attend_own)
    pl.semaphore_wait(barrier, len(greet))
    for distance in range(1, REACH + 1):
        doc_copy(distance).start()

    def send_own(half):
        for head in reversed(range(ONWARD[half], KEY_VALUE_HEADS)):
            block_copy(MINUS, REACH + 1, head).start()
        for head in range(ONWARD[half]):
            block_copy(PLUS, 1, head).start()

    pl.when(in_first_half)(lambda: send_own(0))
    pl.when(jnp.logical_not(in_first_half))(lambda: send_own(1))
    pl.when(jnp.logical_not(early))(attend_own)
    def follow(half):
        order = orders[half]
        blocks = [step[2:] for step in order if step[1] == "block"]
        work, waiting, passed = [], HOLD, set()
        unfinished = {head: [] for head in range(KEY_VALUE_HEADS)}
        for head in range(KEY_VALUE_HEADS):
            ways = {PLUS if head < onward else MINUS for onward in ONWARD}
            unfinished[head] = list(EITHER[half] if len(ways) == 2 else STEPS[ways.pop()])
        sent = [(PLUS, 1, head) for head in range(ONWARD[half])]
        sent += [(MINUS, REACH + 1, head) for head in range(ONWARD[half], KEY_VALUE_HEADS)]
        for step in order:
            if step[1] == "doc":
                doc_copy(step[2]).wait_recv()
                fill_bias(step[2])
                waiting = 0 if step[2] == REACH else waiting
                continue
            way, distance, head = step[2:]
            onward = distance + 1 if way == PLUS else distance - 1

            def arrived():
                block_copy(way, distance, head).wait_recv()
                if 1 <= onward <= REACH:
                    block_copy(way, onward, head).start()

            by_way(half, way, distance, head, arrived)
            passed.add((way, distance, head))
            for pair in list(unfinished[head]):
                if not any((w, d, head) in blocks and (w, d, head) not in passed for w in (PLUS, MINUS) for d in pair):
                    unfinished[head].remove(pair)
                    work.append((head, pair, False, not unfinished[head]))
            if work and not waiting:
                attend(*work.pop(0))
        for item in work:
            attend(*item)
        for copy in sent:
            block_copy(*copy).wait_send()
        for way, distance, head in blocks:
            onward = distance + 1 if way == PLUS else distance - 1
            if 1 <= onward <= REACH:
                by_way(half, way, distance, head, lambda: block_copy(way, onward, head).wait_send())

    pl.when(in_first_half)(lambda: follow(0))
    pl.when(jnp.logical_not(in_first_half))(lambda: follow(1))
    for distance in range(1, REACH + 1):
        doc_copy(distance).wait_send()


def on_device(seq_size, device_count, queries, keys, values, doc_ids):
    tokens = queries.shape[0]
    orders = [schedule(half, *times) for half, times in enumerate(TIMES)]
    pair = (tokens, HEAD_SIZE)
    links = (REACH + 1, KEY_VALUE_HEADS)
    return pl.pallas_call(
        functools.partial(kernel, seq_size, device_count, orders),
        out_shape=jax.ShapeDtypeStruct(queries.shape, jnp.bfloat16),
        in_specs=[
            pl.BlockSpec(memory_space=pltpu.HBM),
            pl.BlockSpec(memory_space=pltpu.HBM),
            pl.BlockSpec(memory_space=pltpu.HBM),
            pl.BlockSpec(memory_space=pltpu.HBM),
        ],
        out_specs=pl.BlockSpec(memory_space=pltpu.VMEM),
        scratch_shapes=[
            pltpu.VMEM((REACH + 1, KEY_VALUE_HEADS, 2, *pair), jnp.bfloat16),
            pltpu.VMEM((KEY_VALUE_HEADS - min(ONWARD), 2, *pair), jnp.bfloat16),
            pltpu.VMEM(queries.shape, jnp.bfloat16),
            pltpu.VMEM((1, tokens), jnp.int32),
            pltpu.VMEM((REACH + 1, 8, tokens), jnp.int32),
            pltpu.VMEM((REACH + 1, tokens, tokens), jnp.float32),
            pltpu.VMEM((KEY_VALUE_HEADS, 1, GROUP * tokens), jnp.float32),
            pltpu.VMEM((KEY_VALUE_HEADS, 1, GROUP * tokens), jnp.float32),
            pltpu.VMEM((KEY_VALUE_HEADS, HEAD_SIZE, GROUP * tokens), jnp.float32),
            pltpu.SemaphoreType.DMA((KEY_VALUE_HEADS, 2)),
            pltpu.SemaphoreType.DMA,
            pltpu.SemaphoreType.DMA,
            pltpu.SemaphoreType.DMA((2, *links)),
            pltpu.SemaphoreType.DMA(links),
            pltpu.SemaphoreType.DMA((REACH,)),
            pltpu.SemaphoreType.DMA((REACH,)),
        ],
        compiler_params=pltpu.CompilerParams(
            collective_id=0, has_side_effects=True, vmem_limit_bytes=VMEM_BYTES
        ),
    )(*(pltpu.with_memory_space_constraint(x, pltpu.HBM) for x in (queries, keys, values, doc_ids.reshape(1, tokens))))


def solution(mesh):
    seq_size = mesh.shape["seq"]
    spec = P(("dp", "seq"), None)
    return jax.shard_map(
        functools.partial(on_device, seq_size, mesh.shape["dp"] * seq_size),
        mesh=mesh,
        in_specs=(spec, spec, spec, P(("dp", "seq"))),
        out_specs=spec,
        check_vma=False,
    )
```

```python
import functools

import jax
import jax.numpy as jnp
from jax import lax
from jax.experimental import pallas as pl
from jax.experimental.pallas import tpu as pltpu
from jax.sharding import PartitionSpec as P

QUERY_HEADS = 64
KEY_VALUE_HEADS = 8
GROUP = QUERY_HEADS // KEY_VALUE_HEADS
HEAD_SIZE = 128
LONGEST_DOCUMENT = 512
VMEM_BYTES = 40 << 20
HOLD = 1
LINE = 8
TIMES = (((3.9, 1.4, 5.3), (7.0, 1.4, 4.2, 0.0), 8.0), ((3.9, 1.4, 6), (7.0, 1.4, 4.2, 3.0), 8.0))


def own_first(dp, seq):
    return lax.rem(seq, LINE) < 3


MESH = pl.DeviceIdType.MESH
SCORE_SCALE = HEAD_SIZE**-0.5 * 1.4426950408889634

ONWARD = (6, 5)
REACH = 4
PLUS, MINUS = 0, 1
STEPS = {PLUS: ((1, 2), (3, 4)), MINUS: ((4, 3), (2, 1))}
EITHER = (((4, 3), (2, 1)), ((2, 3), (1, 4)))


def sender_halves(half, distance):
    places = range(half * LINE // 2, (half + 1) * LINE // 2)
    return {(place - distance) % LINE * 2 // LINE for place in places}


def schedule(half, plus, minus, doc):
    steps = [(doc + 0.1 * distance, "doc", distance) for distance in range(1, REACH + 1)]
    for distance in range(1, REACH + 1):
        for head in range(max(ONWARD[sender] for sender in sender_halves(half, distance))):
            steps.append((plus[0] + plus[1] * ((distance - 1) * plus[2] + head), "block", PLUS, distance, head))
    for distance in range(1, REACH + 2):
        for head in range(min(ONWARD[sender] for sender in sender_halves(half, distance)), KEY_VALUE_HEADS):
            index, stage = KEY_VALUE_HEADS - 1 - head, REACH + 1 - distance
            time = minus[0] + minus[1] * index + minus[2] * stage + (minus[3] if stage else 0.0)
            steps.append((time, "block", MINUS, distance, head))
    return sorted(steps)


def kernel(
    seq_size, device_count, orders, queries, keys, values, docs, out,
    pairs, transit, query_rows, own_docs, doc_rows, bias, top, total, partial,
    local_sem, query_sem, doc_sem, send_sem, recv_sem, doc_send, doc_recv,
):
    me = lax.axis_index("dp") * seq_size + lax.axis_index("seq")

    def block_device(step):
        block = lax.rem(me + (step + device_count), device_count)
        return (block // seq_size, lax.rem(block, seq_size))

    right, left, ahead, behind = (block_device(s) for s in (1, -1, REACH + 1, -REACH - 1))
    greet = (right, left, behind, *(block_device(-distance) for distance in range(2, REACH + 1)))
    barrier = pltpu.get_barrier_semaphore()
    for device in greet:
        pl.semaphore_signal(barrier, inc=1, device_id=device, device_id_type=MESH)
    own = [pltpu.make_async_copy(docs, own_docs, doc_sem)]
    own[0].start()
    landing = {}
    for head in (*reversed(range(min(ONWARD), KEY_VALUE_HEADS)), *range(min(ONWARD))):
        for part, ref in enumerate((keys, values)):
            columns = ref.at[:, pl.ds(head * HEAD_SIZE, HEAD_SIZE)]
            own.append(pltpu.make_async_copy(columns, pairs.at[0, head, part], local_sem.at[head, part]))
            own[-1].start()
            landing.setdefault(head, []).append(own[-1])
    query_copy = pltpu.make_async_copy(queries, query_rows, query_sem)
    query_copy.start()
    own.pop(0).wait()
    doc_rows[0] = jnp.broadcast_to(own_docs[...], doc_rows.shape[1:])

    def remote(source, target, sent, received, device):
        return pltpu.make_async_remote_copy(
            src_ref=source, dst_ref=target, send_sem=sent, recv_sem=received, device_id=device, device_id_type=MESH
        )

    place = lax.rem(lax.axis_index("seq"), LINE)
    in_first_half = place < LINE // 2

    def by_way(half, way, distance, head, action):
        ways = {sender: PLUS if head < ONWARD[sender] else MINUS for sender in sender_halves(half, distance)}
        if set(ways.values()) == {way}:
            action()
        elif way in ways.values():
            first = lax.rem(place - distance + LINE, LINE) < LINE // 2
            pl.when(first if ways[0] == way else jnp.logical_not(first))(action)

    def block_copy(way, distance, head):
        sems = (send_sem.at[way, distance - 1, head], recv_sem.at[distance - 1, head])
        if way == PLUS:
            return remote(pairs.at[distance - 1, head], pairs.at[distance, head], *sems, right)
        if distance > REACH:
            return remote(pairs.at[0, head], transit.at[head - min(ONWARD)], *sems, ahead)
        source = transit.at[head - min(ONWARD)] if distance == REACH else pairs.at[distance + 1, head]
        return remote(source, pairs.at[distance, head], *sems, left)

    def doc_copy(distance):
        return remote(
            doc_rows.at[0], doc_rows.at[distance], doc_send.at[distance - 1], doc_recv.at[distance - 1], block_device(distance)
        )

    def attend(head, blocks, first, last):
        tokens = query_rows.shape[0]
        key_rows = jnp.concatenate([pairs[d, head, 0] for d in blocks], axis=0)
        value_rows = jnp.concatenate([pairs[d, head, 1] for d in blocks], axis=0)
        mask = jnp.concatenate([bias[d] for d in blocks], axis=0)
        columns = [pl.ds(pl.multiple_of((head * GROUP + g) * HEAD_SIZE, HEAD_SIZE), HEAD_SIZE) for g in range(GROUP)]
        rows = jnp.concatenate([query_rows[:, column] for column in columns], axis=0)
        scores = lax.dot_general(key_rows, rows, (((1,), (1,)), ((), ())), preferred_element_type=jnp.float32)
        scores = scores * SCORE_SCALE + jnp.concatenate([mask] * GROUP, axis=1)
        highest = jnp.max(scores, axis=0, keepdims=True)
        if not first:
            highest = jnp.maximum(highest, top[head])
        weight = jnp.exp2(scores - highest)
        sums = jnp.sum(weight, axis=0, keepdims=True)
        mixed = lax.dot_general(
            value_rows, weight.astype(jnp.bfloat16), (((0,), (0,)), ((), ())), preferred_element_type=jnp.float32
        )
        if not first:
            shrink = jnp.exp2(top[head] - highest)
            sums = sums + total[head] * shrink
            mixed = mixed + partial[head] * shrink
        if not last:
            top[head], total[head], partial[head] = highest, sums, mixed
            return
        mixed = mixed / sums
        for g, column in enumerate(columns):
            out[:, column] = mixed[:, g * tokens : (g + 1) * tokens].T.astype(jnp.bfloat16)

    def fill_bias(distance):
        tokens = query_rows.shape[0]
        square = (tokens, tokens)
        same = jnp.broadcast_to(doc_rows[distance, 0:1], square).T == jnp.broadcast_to(own_docs[...], square)
        if distance == 0:
            key, query = (lax.broadcasted_iota(jnp.int32, square, axis) for axis in (0, 1))
            same = same & (key <= query)
        else:
            same = same & (jnp.full(square, me, jnp.int32) >= distance)
        bias[distance] = jnp.where(same, 0.0, -jnp.inf)

    def attend_own():
        query_copy.wait()
        fill_bias(0)
        pl.loop(0, KEY_VALUE_HEADS)(lambda head: attend(head, (0,), True, False))

    def wait_own(heads):
        for head in heads:
            for copy in landing[head]:
                copy.wait()

    pl.when(in_first_half)(lambda: wait_own(range(KEY_VALUE_HEADS)))
    early = own_first(lax.axis_index("dp"), lax.axis_index("seq"))
    pl.when(early)(attend_own)
    pl.semaphore_wait(barrier, len(greet))
    for distance in range(1, REACH + 1):
        doc_copy(distance).start()

    def send_own(half):
        for head in reversed(range(ONWARD[half], KEY_VALUE_HEADS)):
            if half == 1:
                wait_own([head])
            block_copy(MINUS, REACH + 1, head).start()
        for head in range(ONWARD[half]):
            if half == 1:
                wait_own([head])
            block_copy(PLUS, 1, head).start()

    pl.when(in_first_half)(lambda: send_own(0))
    pl.when(jnp.logical_not(in_first_half))(lambda: send_own(1))
    pl.when(jnp.logical_not(early))(attend_own)
    def follow(half):
        order = orders[half]
        blocks = [step[2:] for step in order if step[1] == "block"]
        work, waiting, passed = [], HOLD, set()
        unfinished = {head: [] for head in range(KEY_VALUE_HEADS)}
        for head in range(KEY_VALUE_HEADS):
            ways = {PLUS if head < onward else MINUS for onward in ONWARD}
            unfinished[head] = list(EITHER[half] if len(ways) == 2 else STEPS[ways.pop()])
        sent = [(PLUS, 1, head) for head in range(ONWARD[half])]
        sent += [(MINUS, REACH + 1, head) for head in range(ONWARD[half], KEY_VALUE_HEADS)]
        for step in order:
            if step[1] == "doc":
                doc_copy(step[2]).wait_recv()
                fill_bias(step[2])
                waiting = 0 if step[2] == REACH else waiting
                continue
            way, distance, head = step[2:]
            onward = distance + 1 if way == PLUS else distance - 1

            def arrived():
                block_copy(way, distance, head).wait_recv()
                if 1 <= onward <= REACH:
                    block_copy(way, onward, head).start()

            by_way(half, way, distance, head, arrived)
            passed.add((way, distance, head))
            for pair in list(unfinished[head]):
                if not any((w, d, head) in blocks and (w, d, head) not in passed for w in (PLUS, MINUS) for d in pair):
                    unfinished[head].remove(pair)
                    work.append((head, pair, False, not unfinished[head]))
            if work and not waiting:
                attend(*work.pop(0))
        for item in work:
            attend(*item)
        for copy in sent:
            block_copy(*copy).wait_send()
        for way, distance, head in blocks:
            onward = distance + 1 if way == PLUS else distance - 1
            if 1 <= onward <= REACH:
                by_way(half, way, distance, head, lambda: block_copy(way, onward, head).wait_send())

    pl.when(in_first_half)(lambda: follow(0))
    pl.when(jnp.logical_not(in_first_half))(lambda: follow(1))
    for distance in range(1, REACH + 1):
        doc_copy(distance).wait_send()


def on_device(seq_size, device_count, queries, keys, values, doc_ids):
    tokens = queries.shape[0]
    orders = [schedule(half, *times) for half, times in enumerate(TIMES)]
    pair = (tokens, HEAD_SIZE)
    links = (REACH + 1, KEY_VALUE_HEADS)
    return pl.pallas_call(
        functools.partial(kernel, seq_size, device_count, orders),
        out_shape=jax.ShapeDtypeStruct(queries.shape, jnp.bfloat16),
        in_specs=[
            pl.BlockSpec(memory_space=pltpu.HBM),
            pl.BlockSpec(memory_space=pltpu.HBM),
            pl.BlockSpec(memory_space=pltpu.HBM),
            pl.BlockSpec(memory_space=pltpu.HBM),
        ],
        out_specs=pl.BlockSpec(memory_space=pltpu.VMEM),
        scratch_shapes=[
            pltpu.VMEM((REACH + 1, KEY_VALUE_HEADS, 2, *pair), jnp.bfloat16),
            pltpu.VMEM((KEY_VALUE_HEADS - min(ONWARD), 2, *pair), jnp.bfloat16),
            pltpu.VMEM(queries.shape, jnp.bfloat16),
            pltpu.VMEM((1, tokens), jnp.int32),
            pltpu.VMEM((REACH + 1, 8, tokens), jnp.int32),
            pltpu.VMEM((REACH + 1, tokens, tokens), jnp.float32),
            pltpu.VMEM((KEY_VALUE_HEADS, 1, GROUP * tokens), jnp.float32),
            pltpu.VMEM((KEY_VALUE_HEADS, 1, GROUP * tokens), jnp.float32),
            pltpu.VMEM((KEY_VALUE_HEADS, HEAD_SIZE, GROUP * tokens), jnp.float32),
            pltpu.SemaphoreType.DMA((KEY_VALUE_HEADS, 2)),
            pltpu.SemaphoreType.DMA,
            pltpu.SemaphoreType.DMA,
            pltpu.SemaphoreType.DMA((2, *links)),
            pltpu.SemaphoreType.DMA(links),
            pltpu.SemaphoreType.DMA((REACH,)),
            pltpu.SemaphoreType.DMA((REACH,)),
        ],
        compiler_params=pltpu.CompilerParams(
            collective_id=0, has_side_effects=True, vmem_limit_bytes=VMEM_BYTES
        ),
    )(*(pltpu.with_memory_space_constraint(x, pltpu.HBM) for x in (queries, keys, values, doc_ids.reshape(1, tokens))))


def solution(mesh):
    seq_size = mesh.shape["seq"]
    spec = P(("dp", "seq"), None)
    return jax.shard_map(
        functools.partial(on_device, seq_size, mesh.shape["dp"] * seq_size),
        mesh=mesh,
        in_specs=(spec, spec, spec, P(("dp", "seq"))),
        out_specs=spec,
        check_vma=False,
    )
```
